32 devices in a mesh: leaf: 4 (over z), row: 8 (over y, x, core).
Axes of the slice: x: 2, y: 2, z: 4, core: 2. Of those that a mesh axis runs over, the one named last changes fastest.
Arguments:
- sub_factors: float32 [4, 2048, 512], P('leaf', 'row'), may hold values from -1 to 4, as said below
- row_values: float32 [4, 2048, 128], P('leaf', 'row'), may hold values from -1.2 to 1.2
- row_pattern: int32 [4, 32, 2], P('leaf', 'row'), may hold values 0 or 1
Outputs:
- level4_rows: float32 [2048, 512], P('row', 'leaf')
- level3_rows: float32 [256, 1792], P(('leaf', 'row'))
The draws below stay inside these ranges and needn't reach their ends.
Inputs may be any that keep to these rules, and one draw needn't show every extreme that they name: sub_factors[i, c, r] is zero for c < r and positive for c == r.
All inputs are finite; a program needn't handle non-finite values. No bound on the sum of `row_pattern` on one device may be relied on, other than what follows from the above.
Results may differ from the reference program's by a relative error of at most 0.0003.
Values sent between devices are 32-bit elements; how exact they have to be, the bound alone decides.
A program may use at most 64 MiB of HBM per device.

```python
import math
import jax
import jax.numpy as jnp
from jax import lax

FRONT = 2048
PANEL = 64
ROWS_GROUP = 128
SEP = 256
SUBTREES = 4


def draw_sub_factors(key, part):
    key_diag, key_off = jax.random.split(key)
    full_shape = (SUBTREES, FRONT, 2 * SEP)
    col_index = lax.broadcasted_iota(jnp.int32, full_shape, 1)
    row_index = lax.broadcasted_iota(jnp.int32, full_shape, 2)
    off_scale = 0.4 / math.sqrt(FRONT)
    off_entries = jnp.clip(jax.random.normal(key_off, full_shape, jnp.float32), -6.0, 6.0) * off_scale
    diagonal = jax.random.uniform(key_diag, full_shape, jnp.float32, 1.0, 2.0)
    upper_part = jnp.where(col_index > row_index, off_entries, 0.0)
    return jnp.where(col_index == row_index, diagonal, upper_part).astype(jnp.float32)


def with_ends(drawn, stream_key, smallest, top_value):
    index_at = [jax.random.randint(jax.random.fold_in(stream_key, axis), (), 0, length) for axis, length in enumerate(drawn.shape)]
    longest = drawn.shape.index(max(drawn.shape))
    neighbour = index_at[:longest] + [(index_at[longest] + 1) % drawn.shape[longest]] + index_at[longest + 1:]
    return drawn.at[tuple(index_at)].set(smallest).at[tuple(neighbour)].set(top_value)


def steps_of(key, shape, pieces, smallest, top_value):
    loudness = 1.0
    for position, blocks in pieces:
        steps = jax.random.uniform(jax.random.fold_in(jax.random.fold_in(key, 6), position), (blocks,), jnp.float32, smallest / len(pieces), top_value / len(pieces))
        loudness = loudness * jnp.repeat(jnp.exp(steps), shape[position] // blocks).reshape((-1,) + (1,) * (len(shape) - 1 - position))
    return loudness


def noise(own_key, shape, deviation, reach, cuts=(), held_as=jnp.bfloat16):
    factor_of = steps_of(own_key, shape, cuts, -0.22, 0.18) if cuts else 1.0
    values = jax.random.normal(own_key, shape, jnp.float32) * deviation * factor_of
    return jnp.minimum(jnp.maximum(values, -reach), reach).astype(held_as)


def setup_inputs(seed: int = 0) -> dict:
    keys = jax.random.split(jax.random.key(seed), 4)
    return {
        "sub_factors": draw_sub_factors(jax.random.fold_in(keys[3], 71), 0),
        "row_values": noise(keys[1], (SUBTREES, FRONT, ROWS_GROUP), 0.2, 1.2, ((0, 4), (1, 8)), jnp.float32),
        "row_pattern": with_ends((jax.random.randint(keys[2], (SUBTREES, FRONT // PANEL, ROWS_GROUP // PANEL), 0, 2) < 1).astype(jnp.int32), jax.random.fold_in(keys[2], 1), 0, 1),
    }


exact_dots = lax.Precision.HIGHEST

def masked_rows(values, pattern):
    row_blocks = pattern.shape[0]
    col_blocks = pattern.shape[1]
    blocks = values.reshape(row_blocks, PANEL, col_blocks, PANEL)
    flags = pattern[:, None, :, None].astype(values.dtype)
    return (blocks * flags).reshape(values.shape)

def pivot_rows(stacked_rows):
    basis, upper = jnp.linalg.qr(stacked_rows[:, :SEP])
    signs = jnp.where(jnp.diagonal(upper) < 0, -1.0, 1.0).astype(stacked_rows.dtype)
    basis = basis * signs[None, :]
    rows_out = jnp.dot(basis.T.astype(jnp.float32), stacked_rows.astype(jnp.float32), precision=exact_dots, preferred_element_type=jnp.float32)
    remainder = stacked_rows[:, SEP:] - jnp.dot(basis.astype(jnp.float32), rows_out[:, SEP:].astype(jnp.float32), precision=exact_dots, preferred_element_type=jnp.float32)
    return (rows_out, remainder)

def reference(sub_factors, row_values, row_pattern):
    factor_rows = jnp.swapaxes(sub_factors, 1, 2)
    value_rows = jnp.swapaxes(row_values, 1, 2)
    pattern_rows = jnp.swapaxes(row_pattern, 1, 2)
    level_four = []
    contributions = []
    for front in range(SUBTREES // 2):
        left_child = 2 * front
        right_child = 2 * front + 1
        stacked_rows = jnp.concatenate([factor_rows[left_child, :SEP], factor_rows[right_child, :SEP], masked_rows(value_rows[left_child], pattern_rows[left_child]), masked_rows(value_rows[right_child], pattern_rows[right_child])], axis=0)
        rows_out, remainder = pivot_rows(stacked_rows)
        level_four.append(rows_out)
        contributions.append(jnp.concatenate([remainder, factor_rows[left_child, SEP:2 * SEP, SEP:], factor_rows[right_child, SEP:2 * SEP, SEP:]], axis=0))
    level_three = []
    for front in range(SUBTREES // 4):
        stacked_rows = jnp.concatenate([contributions[2 * front], contributions[2 * front + 1]], axis=0)
        rows_out, remainder = pivot_rows(stacked_rows)
        level_three.append(rows_out)
    return (jnp.concatenate(level_four, axis=0).T, jnp.concatenate(level_three, axis=0))
```

```python
import functools

import jax
import jax.numpy as jnp
from jax import lax
from jax.experimental import pallas as pl
from jax.experimental.pallas import tpu as pltpu
from jax.sharding import PartitionSpec as P

PANEL = 64
SEP = 256
GROUP = 4
MESH = pl.DeviceIdType.MESH
exact_dots = lax.Precision.HIGHEST


def dot(left, right, left_dim, right_dim):
    return lax.dot_general(
        left,
        right,
        (((left_dim,), (right_dim,)), ((), ())),
        precision=exact_dots,
        preferred_element_type=jnp.float32,
    )


def small_factor(augmented):
    count = PANEL
    sub = lax.broadcasted_iota(jnp.int32, (8, 2 * PANEL), 0)
    live = augmented
    done = []
    for start in range(0, count, GROUP):
        offset = start % 8
        if start and offset == 0:
            done.append(live[:8])
            live = live[8:]
        cols = [
            jnp.broadcast_to(live[:, start + a : start + a + 1], live.shape) for a in range(GROUP)
        ]
        rows = [live[offset + a : offset + a + 1] for a in range(GROUP)]
        diag = [[cols[b][offset + a : offset + a + 1] for b in range(GROUP)] for a in range(GROUP)]
        factors = []
        for a in range(GROUP):
            inverse = 1.0 / diag[a][a]
            factors.append(cols[a] * inverse)
            for i in range(a + 1, GROUP):
                multiple = diag[i][a] * inverse
                rows[i] = rows[i] - multiple * rows[a]
                cols[i] = cols[i] - factors[a] * diag[a][i]
                for b in range(a + 1, GROUP):
                    diag[i][b] = diag[i][b] - multiple * diag[a][b]
        updated = live
        for a in range(GROUP):
            updated = updated - factors[a] * rows[a]
        top = jnp.where(sub >= offset + GROUP, updated[:8], live[:8])
        for a in range(GROUP):
            top = jnp.where(sub == offset + a, rows[a], top)
        live = jnp.concatenate([top, updated[8:]], axis=0) if live.shape[0] > 8 else top
    out = jnp.concatenate(done + [live], axis=0)
    row = lax.broadcasted_iota(jnp.int32, out.shape, 0)
    col = lax.broadcasted_iota(jnp.int32, out.shape, 1)
    pivots = jnp.sum(jnp.where(row == col, out, 0.0), axis=1, keepdims=True)
    return out * lax.rsqrt(pivots)


def factor_inverse(aug, gram):
    row = lax.broadcasted_iota(jnp.int32, (SEP, SEP), 0)
    col = lax.broadcasted_iota(jnp.int32, (SEP, SEP), 1)
    eye = jnp.where(row == col, 1.0, 0.0).astype(jnp.float32)
    aug[:, :SEP] = gram
    aug[:, SEP:] = eye
    for low in range(0, SEP, PANEL):
        high = low + PANEL
        square = aug[low:high, low:high]
        inverse = small_factor(jnp.concatenate([square, eye[:PANEL, :PANEL]], axis=1))[:, PANEL:]
        rows = dot(inverse, aug[low:high, :], 1, 0)
        aug[low:high, :] = rows
        if high < SEP:
            aligned = high // 128 * 128
            update = dot(rows[:, aligned:SEP], rows, 0, 0)
            aug[high:SEP, :] = aug[high:SEP, :] - update[high - aligned :]
    return aug[:, SEP:]


def kernel(
    n_row,
    own,
    four,
    three,
    piv,
    gs,
    gr,
    xs,
    xr,
    hs,
    hr,
    ys,
    yr,
    mix,
    half,
    quarter,
    halves,
    quarters,
    aug,
    raw_s,
    raw_r,
    relay_s,
    g_s,
    g_r,
    x_s,
    x_r,
    hy_s,
    hy_r,
    mix_s,
    half_s,
    quarter_s,
    down_r,
):
    leaf = lax.axis_index("leaf")
    me = lax.axis_index("row")
    width = own.shape[0]
    owners = 2 * SEP // width
    near = leaf + 1 - 2 * lax.rem(leaf, 2)
    far = leaf + 2 - 4 * lax.rem(leaf // 2, 2)
    sibling = me + 1 - 2 * lax.rem(me, 2)
    tall = own.shape[1]
    short = tall - SEP

    barrier = pltpu.get_barrier_semaphore()
    for step in range(1, n_row):
        pl.semaphore_signal(
            barrier,
            inc=1,
            device_id={"leaf": leaf, "row": lax.rem(me + step, n_row)},
            device_id_type=MESH,
        )
    for other in (near, far):
        pl.semaphore_signal(
            barrier, inc=1, device_id={"leaf": other, "row": me}, device_id_type=MESH
        )
    pl.semaphore_wait(barrier, n_row + 1)

    def remote(src, dst, send, recv, to_leaf, to_row):
        return pltpu.make_async_remote_copy(
            src_ref=src,
            dst_ref=dst,
            send_sem=send,
            recv_sem=recv,
            device_id={"leaf": to_leaf, "row": to_row},
            device_id_type=MESH,
        )

    def rows_of(block):
        return short if block * width < SEP else tall

    def raw(block, target):
        count = rows_of(block)
        return remote(
            own.at[:, pl.ds(0, count)],
            piv.at[block, :, pl.ds(0, count)],
            raw_s.at[target],
            raw_r.at[block],
            leaf,
            target,
        )

    def relay(block):
        view = piv.at[block, :, pl.ds(0, rows_of(block))]
        return remote(view, view, relay_s.at[block], raw_r.at[block], leaf, sibling)

    def raw_targets(block):
        chip, core = block // 2, block % 2
        others = [2 * q + core for q in range(n_row // 2) if q != chip]
        return [2 * chip + 1 - core] + others

    for block in range(owners):

        @pl.when(me == block)
        def _():
            for target in raw_targets(block):
                raw(block, target).start()
            piv[block] = own[...]

    for block in range(owners):

        @pl.when(me != block)
        def _():
            relay(block).wait_recv()

            @pl.when(lax.rem(me, 2) == block % 2)
            def _():
                relay(block).start()

    def pivots(first, last, count):
        blocks = [piv[b, :, :count] for b in range(first, last)]
        return blocks[0] if len(blocks) == 1 else jnp.concatenate(blocks, axis=0)

    def g_copy(i):
        return remote(gs.at[i], gr.at[i], g_s.at[i], g_r.at[i], near, me)

    def x_copy(i):
        return remote(xs.at[i], xr.at[i], x_s.at[i], x_r.at[i], near, me)

    h_copy = remote(hs, hr, hy_s.at[0], hy_r.at[0], far, me)
    y_copy = remote(ys, yr, hy_s.at[1], hy_r.at[1], far, me)
    which_half = lax.rem(leaf, 2)
    which_quarter = lax.rem(leaf, 4)

    def mix_copy(target):
        return remote(mix, mix, mix_s.at[target], down_r.at[0], leaf, target)

    def half_copy(target):
        return remote(
            halves.at[which_half], half, half_s.at[target], down_r.at[1], leaf, target
        )

    def quarter_copy(target):
        return remote(
            quarters.at[which_quarter], quarter, quarter_s.at[target], down_r.at[2], leaf, target
        )

    mid = owners // 2

    @pl.when(me == 0)
    def _():
        first = pivots(0, mid, short)
        gs[0] = dot(first, first, 1, 1)
        g_copy(0).start()
        second = pivots(mid, owners, tall)
        gs[1] = dot(first, second[:, :short], 1, 1)
        g_copy(1).start()
        gs[2] = dot(second, second, 1, 1)
        g_copy(2).start()

    xs[0] = dot(own[:, :short], pivots(0, mid, short), 1, 1)
    x_copy(0).start()
    xs[1] = dot(own[...], pivots(mid, owners, tall), 1, 1)
    x_copy(1).start()

    @pl.when(me == 0)
    def _():
        g_copy(0).wait_recv()
        inverse = factor_inverse(aug, gs[0] + gr[0])
        g_copy(1).wait_recv()
        pivot_rows = dot(inverse, gs[1] + gr[1], 1, 0)
        g_copy(2).wait_recv()
        hs[...] = gs[2] + gr[2] - dot(pivot_rows, pivot_rows, 0, 0)
        h_copy.start()
        mix[...] = dot(inverse, pivot_rows, 0, 0)
        for target in range(1, n_row):
            mix_copy(target).start()
        halves[0] = inverse[: SEP // 2]
        halves[1] = inverse[SEP // 2 :]
        for target in range(1, n_row):
            half_copy(target).start()

    @pl.when(me != 0)
    def _():
        mix_copy(0).wait_recv()

    x_copy(0).wait_recv()
    x_copy(1).wait_recv()
    cross_four = xs[0] + xr[0]
    ys[...] = xs[1] + xr[1] - dot(cross_four, mix[...], 1, 0)
    y_copy.start()

    @pl.when(me == 0)
    def _():
        h_copy.wait_recv()
        inverse = factor_inverse(aug, hs[...] + hr[...])
        for i in range(4):
            quarters[i] = inverse[i * PANEL : (i + 1) * PANEL]
        for target in range(1, n_row):
            quarter_copy(target).start()
        half[...] = halves[which_half]
        quarter[...] = quarters[which_quarter]

    @pl.when(me != 0)
    def _():
        half_copy(0).wait_recv()

    four[...] = dot(xs[0] + xr[0], half[...], 1, 1)
    y_copy.wait_recv()

    @pl.when(me != 0)
    def _():
        quarter_copy(0).wait_recv()

    three[...] = dot(ys[...] + yr[...], quarter[...], 1, 1)

    for block in range(owners):

        @pl.when(me == block)
        def _():
            for target in raw_targets(block):
                raw(block, target).wait_send()

        @pl.when(jnp.logical_and(me != block, lax.rem(me, 2) == block % 2))
        def _():
            relay(block).wait_send()

    x_copy(0).wait_send()
    x_copy(1).wait_send()
    y_copy.wait_send()

    @pl.when(me == 0)
    def _():
        for i in range(3):
            g_copy(i).wait_send()
        h_copy.wait_send()
        for target in range(1, n_row):
            mix_copy(target).wait_send()
            half_copy(target).wait_send()
            quarter_copy(target).wait_send()


def fronts(own, n_row):
    width, tall = own.shape
    owners = 2 * SEP // width
    f32 = jnp.float32
    square = pltpu.VMEM((SEP, SEP), f32)
    dma = pltpu.SemaphoreType.DMA
    vmem = pl.BlockSpec(memory_space=pltpu.VMEM)
    return pl.pallas_call(
        functools.partial(kernel, n_row),
        out_shape=(
            jax.ShapeDtypeStruct((width, SEP // 2), f32),
            jax.ShapeDtypeStruct((width, SEP // 4), f32),
        ),
        in_specs=[vmem],
        out_specs=(vmem, vmem),
        scratch_shapes=[
            pltpu.VMEM((owners, width, tall), f32),
            pltpu.VMEM((3, SEP, SEP), f32),
            pltpu.VMEM((3, SEP, SEP), f32),
            pltpu.VMEM((2, width, SEP), f32),
            pltpu.VMEM((2, width, SEP), f32),
            square,
            square,
            pltpu.VMEM((width, SEP), f32),
            pltpu.VMEM((width, SEP), f32),
            square,
            pltpu.VMEM((SEP // 2, SEP), f32),
            pltpu.VMEM((SEP // 4, SEP), f32),
            pltpu.VMEM((2, SEP // 2, SEP), f32),
            pltpu.VMEM((4, SEP // 4, SEP), f32),
            pltpu.VMEM((SEP, 2 * SEP), f32),
            dma((n_row,)),
            dma((owners,)),
            dma((owners,)),
            dma((3,)),
            dma((3,)),
            dma((2,)),
            dma((2,)),
            dma((2,)),
            dma((2,)),
            dma((n_row,)),
            dma((n_row,)),
            dma((n_row,)),
            dma((3,)),
        ],
        compiler_params=pltpu.CompilerParams(
            collective_id=0, has_side_effects=True, vmem_limit_bytes=40 * 1024 * 1024
        ),
        name="fronts",
    )(own)


def masked_columns(values, pattern):
    col_blocks = pattern.shape[0]
    row_blocks = pattern.shape[1]
    blocks = values.reshape(col_blocks, PANEL, row_blocks, PANEL)
    flags = pattern[:, None, :, None].astype(jnp.float32)
    return (blocks * flags).reshape(values.shape)


def on_device(n_row, sub_factors, row_values, row_pattern):
    factors = sub_factors[0]
    assembled = masked_columns(row_values[0], row_pattern[0])
    own = jnp.concatenate([factors[:, :SEP], assembled, factors[:, SEP:]], axis=1)
    four_rows, row_piece = fronts(own, n_row)
    spread_rows = lax.all_to_all(row_piece, "row", split_axis=1, concat_axis=0, tiled=True)
    return (four_rows, spread_rows.T[:, SEP:])


def solution(mesh):
    placed = (P("leaf", "row", None), P("leaf", "row", None), P("leaf", "row", None))
    return jax.shard_map(
        functools.partial(on_device, mesh.shape["row"]),
        mesh=mesh,
        in_specs=placed,
        out_specs=(P("row", "leaf"), P(("leaf", "row"), None)),
        check_vma=False,
    )
```

```python
import functools

import jax
import jax.numpy as jnp
from jax import lax
from jax.experimental import pallas as pl
from jax.experimental.pallas import tpu as pltpu
from jax.sharding import PartitionSpec as P

PANEL = 64
SEP = 256
GROUP = 8
MESH = pl.DeviceIdType.MESH
exact_dots = lax.Precision.HIGHEST


def dot(left, right, left_dim, right_dim):
    return lax.dot_general(
        left,
        right,
        (((left_dim,), (right_dim,)), ((), ())),
        precision=exact_dots,
        preferred_element_type=jnp.float32,
    )


def small_factor(augmented):
    count = PANEL
    sub = lax.broadcasted_iota(jnp.int32, (8, 2 * PANEL), 0)
    live = augmented
    done = []
    for start in range(0, count, GROUP):
        offset = start % 8
        if start and offset == 0:
            done.append(live[:8])
            live = live[8:]
        cols = [
            jnp.broadcast_to(live[:, start + a : start + a + 1], live.shape) for a in range(GROUP)
        ]
        rows = [live[offset + a : offset + a + 1] for a in range(GROUP)]
        diag = [[cols[b][offset + a : offset + a + 1] for b in range(GROUP)] for a in range(GROUP)]
        factors = []
        for a in range(GROUP):
            inverse = 1.0 / diag[a][a]
            factors.append(cols[a] * inverse)
            for i in range(a + 1, GROUP):
                multiple = diag[i][a] * inverse
                rows[i] = rows[i] - multiple * rows[a]
                cols[i] = cols[i] - factors[a] * diag[a][i]
                for b in range(a + 1, GROUP):
                    diag[i][b] = diag[i][b] - multiple * diag[a][b]
        updated = live
        for a in range(GROUP):
            updated = updated - factors[a] * rows[a]
        top = jnp.where(sub >= offset + GROUP, updated[:8], live[:8])
        for a in range(GROUP):
            top = jnp.where(sub == offset + a, rows[a], top)
        live = jnp.concatenate([top, updated[8:]], axis=0) if live.shape[0] > 8 else top
    out = jnp.concatenate(done + [live], axis=0)
    row = lax.broadcasted_iota(jnp.int32, out.shape, 0)
    col = lax.broadcasted_iota(jnp.int32, out.shape, 1)
    pivots = jnp.sum(jnp.where(row == col, out, 0.0), axis=1, keepdims=True)
    return out * lax.rsqrt(pivots)


def factor_inverse(aug, gram):
    row = lax.broadcasted_iota(jnp.int32, (SEP, SEP), 0)
    col = lax.broadcasted_iota(jnp.int32, (SEP, SEP), 1)
    eye = jnp.where(row == col, 1.0, 0.0).astype(jnp.float32)
    aug[:, :SEP] = gram
    aug[:, SEP:] = eye
    for low in range(0, SEP, PANEL):
        high = low + PANEL
        square = aug[low:high, low:high]
        inverse = small_factor(jnp.concatenate([square, eye[:PANEL, :PANEL]], axis=1))[:, PANEL:]
        rows = dot(inverse, aug[low:high, :], 1, 0)
        aug[low:high, :] = rows
        if high < SEP:
            aligned = high // 128 * 128
            update = dot(rows[:, aligned:SEP], rows, 0, 0)
            aug[high:SEP, :] = aug[high:SEP, :] - update[high - aligned :]
    return aug[:, SEP:]


def kernel(
    n_row,
    own,
    four,
    three,
    piv,
    gs,
    gr,
    xs,
    xr,
    hs,
    hr,
    ys,
    yr,
    mix,
    half,
    quarter,
    halves,
    quarters,
    aug,
    ts,
    tr,
    raw_s,
    raw_r,
    relay_s,
    onward_s,
    g_s,
    g_r,
    x_s,
    x_r,
    hy_s,
    hy_r,
    mix_s,
    half_s,
    quarter_s,
    down_r,
    spread_s,
    spread_r,
):
    leaf = lax.axis_index("leaf")
    me = lax.axis_index("row")
    width = own.shape[0]
    owners = 2 * SEP // width
    near = leaf + 1 - 2 * lax.rem(leaf, 2)
    far = leaf + 2 - 4 * lax.rem(leaf // 2, 2)
    sibling = me + 1 - 2 * lax.rem(me, 2)
    tall = own.shape[1]
    short = tall - SEP

    barrier = pltpu.get_barrier_semaphore()
    for step in range(1, n_row):
        pl.semaphore_signal(
            barrier,
            inc=1,
            device_id={"leaf": leaf, "row": lax.rem(me + step, n_row)},
            device_id_type=MESH,
        )
    for other in (near, far):
        pl.semaphore_signal(
            barrier, inc=1, device_id={"leaf": other, "row": me}, device_id_type=MESH
        )
    pl.semaphore_wait(barrier, n_row + 1)

    def remote(src, dst, send, recv, to_leaf, to_row):
        return pltpu.make_async_remote_copy(
            src_ref=src,
            dst_ref=dst,
            send_sem=send,
            recv_sem=recv,
            device_id={"leaf": to_leaf, "row": to_row},
            device_id_type=MESH,
        )

    def rows_of(block):
        return short if block * width < SEP else tall

    def part_view(ref, block, part):
        return ref.at[pl.ds(part * (width // 2), width // 2), pl.ds(0, rows_of(block))]

    def raw(block, part, target):
        return remote(
            part_view(own, block, part),
            part_view(piv.at[block], block, part),
            raw_s.at[2 * target + part],
            raw_r.at[2 * block + part],
            leaf,
            target,
        )

    def pass_on(block, part, send, target):
        view = part_view(piv.at[block], block, part)
        return remote(view, view, send, raw_r.at[2 * block + part], leaf, target)

    def relay(block, part):
        return pass_on(block, part, relay_s.at[2 * block + part], sibling)

    def onward(block, part):
        return pass_on(block, part, onward_s.at[block], 6 + block % 2)

    square_plane = n_row == 8

    def raw_sends(block):
        chip, core = block // 2, block % 2
        sends = [(2 * chip + 1 - core, 0), (2 * chip + 1 - core, 1)]
        if square_plane:
            return sends + [(2 + core, 0), (4 + core, 1), (2 + core, 1), (4 + core, 0)]
        others = [2 * q + core for q in range(n_row // 2) if q != chip]
        return sends + [(target, part) for target in others for part in range(2)]

    def arrive(block, part):
        relay(block, part).wait_recv()

        @pl.when(lax.rem(me, 2) == block % 2)
        def _():
            relay(block, part).start()

        if square_plane:

            @pl.when(me == 2 + 2 * part + block % 2)
            def _():
                onward(block, part).start()

    def g_copy(i):
        return remote(gs.at[i], gr.at[i], g_s.at[i], g_r.at[i], near, me)

    mid = owners // 2

    for block in range(owners):

        @pl.when(me == block)
        def _():
            for target, part in raw_sends(block):
                raw(block, part, target).start()
            piv[block] = own[...]
            if block == 0 and mid == 1:
                gs[0] = dot(own[:, :short], own[:, :short], 1, 1)
                g_copy(0).start()

    for block in range(owners):

        @pl.when(me != block)
        def _():
            if square_plane:
                late = me == 4 + block % 2

                @pl.when(late)
                def _():
                    arrive(block, 1)
                    arrive(block, 0)

                @pl.when(jnp.logical_not(late))
                def _():
                    arrive(block, 0)
                    arrive(block, 1)

            else:
                arrive(block, 0)
                arrive(block, 1)

    def pivots(first, last, count):
        blocks = [piv[b, :, :count] for b in range(first, last)]
        return blocks[0] if len(blocks) == 1 else jnp.concatenate(blocks, axis=0)

    def x_copy(i):
        return remote(xs.at[i], xr.at[i], x_s.at[i], x_r.at[i], near, me)

    h_copy = remote(hs, hr, hy_s.at[0], hy_r.at[0], far, me)
    y_copy = remote(ys, yr, hy_s.at[1], hy_r.at[1], far, me)
    which_half = lax.rem(leaf, 2)
    which_quarter = lax.rem(leaf, 4)

    def mix_copy(target):
        return remote(mix, mix, mix_s.at[target], down_r.at[0], leaf, target)

    def half_copy(target):
        return remote(
            halves.at[which_half], half, half_s.at[target], down_r.at[1], leaf, target
        )

    def quarter_copy(target):
        return remote(
            quarters.at[which_quarter], quarter, quarter_s.at[target], down_r.at[2], leaf, target
        )

    @pl.when(me == 0)
    def _():
        first = pivots(0, mid, short)
        if mid > 1:
            gs[0] = dot(first, first, 1, 1)
            g_copy(0).start()
        second = pivots(mid, owners, tall)
        gs[1] = dot(first, second[:, :short], 1, 1)
        g_copy(1).start()
        gs[2] = dot(second, second, 1, 1)
        g_copy(2).start()

    xs[0] = dot(own[:, :short], pivots(0, mid, short), 1, 1)
    x_copy(0).start()
    xs[1] = dot(own[...], pivots(mid, owners, tall), 1, 1)
    x_copy(1).start()

    @pl.when(me == 0)
    def _():
        g_copy(0).wait_recv()
        inverse = factor_inverse(aug, gs[0] + gr[0])
        g_copy(1).wait_recv()
        pivot_rows = dot(inverse, gs[1] + gr[1], 1, 0)
        g_copy(2).wait_recv()
        hs[...] = gs[2] + gr[2] - dot(pivot_rows, pivot_rows, 0, 0)
        h_copy.start()
        mix[...] = dot(inverse, pivot_rows, 0, 0)
        for target in range(1, n_row):
            mix_copy(target).start()
        halves[0] = inverse[: SEP // 2]
        halves[1] = inverse[SEP // 2 :]
        for target in range(1, n_row):
            half_copy(target).start()

    @pl.when(me != 0)
    def _():
        mix_copy(0).wait_recv()

    x_copy(0).wait_recv()
    x_copy(1).wait_recv()
    cross_four = xs[0] + xr[0]
    ys[...] = xs[1] + xr[1] - dot(cross_four, mix[...], 1, 0)
    y_copy.start()

    @pl.when(me == 0)
    def _():
        h_copy.wait_recv()
        inverse = factor_inverse(aug, hs[...] + hr[...])
        for i in range(4):
            quarters[i] = inverse[i * PANEL : (i + 1) * PANEL]
        for target in range(1, n_row):
            quarter_copy(target).start()
        half[...] = halves[which_half]
        quarter[...] = quarters[which_quarter]

    @pl.when(me != 0)
    def _():
        half_copy(0).wait_recv()

    four[...] = dot(xs[0] + xr[0], half[...], 1, 1)
    y_copy.wait_recv()

    @pl.when(me != 0)
    def _():
        quarter_copy(0).wait_recv()

    spread = dot(quarter[...], ys[...] + yr[...], 1, 1)
    share = PANEL // n_row
    for target in range(n_row):
        ts[target] = spread[target * share : (target + 1) * share]

    def spread_copy(source, target):
        return remote(
            ts.at[target], tr.at[source], spread_s.at[target], spread_r.at[source], leaf, target
        )

    for target in range(n_row):

        @pl.when(jnp.logical_and(me >= mid, me != target))
        def _():
            spread_copy(me, target).start()

    for source in range(mid, n_row):

        @pl.when(me == source)
        def _():
            tr[source] = ts[source]

        @pl.when(me != source)
        def _():
            spread_copy(source, source).wait_recv()

    three[...] = jnp.concatenate([tr[source] for source in range(mid, n_row)], axis=1)

    for target in range(n_row):

        @pl.when(jnp.logical_and(me >= mid, me != target))
        def _():
            spread_copy(me, target).wait_send()

    for block in range(owners):

        @pl.when(me == block)
        def _():
            for target, part in raw_sends(block):
                raw(block, part, target).wait_send()

        @pl.when(jnp.logical_and(me != block, lax.rem(me, 2) == block % 2))
        def _():
            for part in range(2):
                relay(block, part).wait_send()

        if square_plane:
            for part in range(2):

                @pl.when(me == 2 + 2 * part + block % 2)
                def _():
                    onward(block, part).wait_send()

    x_copy(0).wait_send()
    x_copy(1).wait_send()
    y_copy.wait_send()

    @pl.when(me == 0)
    def _():
        for i in range(3):
            g_copy(i).wait_send()
        h_copy.wait_send()
        for target in range(1, n_row):
            mix_copy(target).wait_send()
            half_copy(target).wait_send()
            quarter_copy(target).wait_send()


def fronts(own, n_row):
    width, tall = own.shape
    owners = 2 * SEP // width
    f32 = jnp.float32
    square = pltpu.VMEM((SEP, SEP), f32)
    dma = pltpu.SemaphoreType.DMA
    vmem = pl.BlockSpec(memory_space=pltpu.VMEM)
    return pl.pallas_call(
        functools.partial(kernel, n_row),
        out_shape=(
            jax.ShapeDtypeStruct((width, SEP // 2), f32),
            jax.ShapeDtypeStruct((SEP // 4 // n_row, width * n_row - SEP), f32),
        ),
        in_specs=[vmem],
        out_specs=(vmem, vmem),
        scratch_shapes=[
            pltpu.VMEM((owners, width, tall), f32),
            pltpu.VMEM((3, SEP, SEP), f32),
            pltpu.VMEM((3, SEP, SEP), f32),
            pltpu.VMEM((2, width, SEP), f32),
            pltpu.VMEM((2, width, SEP), f32),
            square,
            square,
            pltpu.VMEM((width, SEP), f32),
            pltpu.VMEM((width, SEP), f32),
            square,
            pltpu.VMEM((SEP // 2, SEP), f32),
            pltpu.VMEM((SEP // 4, SEP), f32),
            pltpu.VMEM((2, SEP // 2, SEP), f32),
            pltpu.VMEM((4, SEP // 4, SEP), f32),
            pltpu.VMEM((SEP, 2 * SEP), f32),
            pltpu.VMEM((n_row, SEP // 4 // n_row, width), f32),
            pltpu.VMEM((n_row, SEP // 4 // n_row, width), f32),
            dma((2 * n_row,)),
            dma((2 * owners,)),
            dma((2 * owners,)),
            dma((owners,)),
            dma((3,)),
            dma((3,)),
            dma((2,)),
            dma((2,)),
            dma((2,)),
            dma((2,)),
            dma((n_row,)),
            dma((n_row,)),
            dma((n_row,)),
            dma((3,)),
            dma((n_row,)),
            dma((n_row,)),
        ],
        compiler_params=pltpu.CompilerParams(
            collective_id=0, has_side_effects=True, vmem_limit_bytes=40 * 1024 * 1024
        ),
        name="fronts",
    )(own)


def masked_columns(values, pattern):
    col_blocks = pattern.shape[0]
    row_blocks = pattern.shape[1]
    blocks = values.reshape(col_blocks, PANEL, row_blocks, PANEL)
    flags = pattern[:, None, :, None].astype(jnp.float32)
    return (blocks * flags).reshape(values.shape)


def on_device(n_row, sub_factors, row_values, row_pattern):
    factors = sub_factors[0]
    assembled = masked_columns(row_values[0], row_pattern[0])
    own = jnp.concatenate([factors[:, :SEP], assembled, factors[:, SEP:]], axis=1)
    return fronts(own, n_row)


def solution(mesh):
    placed = (P("leaf", "row", None), P("leaf", "row", None), P("leaf", "row", None))
    return jax.shard_map(
        functools.partial(on_device, mesh.shape["row"]),
        mesh=mesh,
        in_specs=placed,
        out_specs=(P("row", "leaf"), P(("leaf", "row"), None)),
        check_vma=False,
    )
```

```python
import functools

import jax
import jax.numpy as jnp
from jax import lax
from jax.experimental import pallas as pl
from jax.experimental.pallas import tpu as pltpu
from jax.sharding import PartitionSpec as P

PANEL = 64
SEP = 256
GROUP = 8
MESH = pl.DeviceIdType.MESH
exact_dots = lax.Precision.HIGHEST


def dot(left, right, left_dim, right_dim):
    return lax.dot_general(
        left,
        right,
        (((left_dim,), (right_dim,)), ((), ())),
        precision=exact_dots,
        preferred_element_type=jnp.float32,
    )


def small_factor(augmented):
    count = PANEL
    sub = lax.broadcasted_iota(jnp.int32, (8, 2 * PANEL), 0)
    live = augmented
    done = []
    for start in range(0, count, GROUP):
        offset = start % 8
        if start and offset == 0:
            done.append(live[:8])
            live = live[8:]
        cols = [
            jnp.broadcast_to(live[:, start + a : start + a + 1], live.shape) for a in range(GROUP)
        ]
        rows = [live[offset + a : offset + a + 1] for a in range(GROUP)]
        diag = [[cols[b][offset + a : offset + a + 1] for b in range(GROUP)] for a in range(GROUP)]
        factors = []
        for a in range(GROUP):
            inverse = 1.0 / diag[a][a]
            factors.append(cols[a] * inverse)
            for i in range(a + 1, GROUP):
                multiple = diag[i][a] * inverse
                rows[i] = rows[i] - multiple * rows[a]
                cols[i] = cols[i] - factors[a] * diag[a][i]
                for b in range(a + 1, GROUP):
                    diag[i][b] = diag[i][b] - multiple * diag[a][b]
        updated = live
        for a in range(GROUP):
            updated = updated - factors[a] * rows[a]
        top = jnp.where(sub >= offset + GROUP, updated[:8], live[:8])
        for a in range(GROUP):
            top = jnp.where(sub == offset + a, rows[a], top)
        live = jnp.concatenate([top, updated[8:]], axis=0) if live.shape[0] > 8 else top
    out = jnp.concatenate(done + [live], axis=0)
    row = lax.broadcasted_iota(jnp.int32, out.shape, 0)
    col = lax.broadcasted_iota(jnp.int32, out.shape, 1)
    pivots = jnp.sum(jnp.where(row == col, out, 0.0), axis=1, keepdims=True)
    return out * lax.rsqrt(pivots)


def factor_inverse(aug, gram):
    row = lax.broadcasted_iota(jnp.int32, (SEP, SEP), 0)
    col = lax.broadcasted_iota(jnp.int32, (SEP, SEP), 1)
    eye = jnp.where(row == col, 1.0, 0.0).astype(jnp.float32)
    aug[:, :SEP] = gram
    aug[:, SEP:] = eye
    for low in range(0, SEP, PANEL):
        high = low + PANEL
        square = aug[low:high, low:high]
        inverse = small_factor(jnp.concatenate([square, eye[:PANEL, :PANEL]], axis=1))[:, PANEL:]
        rows = dot(inverse, aug[low:high, :], 1, 0)
        aug[low:high, :] = rows
        if high < SEP:
            aligned = high // 128 * 128
            update = dot(rows[:, aligned:SEP], rows, 0, 0)
            aug[high:SEP, :] = aug[high:SEP, :] - update[high - aligned :]
    return aug[:, SEP:]


def kernel(
    n_row,
    own,
    four,
    three,
    piv,
    gs,
    gr,
    xs,
    xr,
    hs,
    hr,
    ys,
    yr,
    mix,
    half,
    quarter,
    halves,
    quarters,
    aug,
    ts,
    tr,
    raw_s,
    raw_r,
    relay_s,
    onward_s,
    g_s,
    g_r,
    x_s,
    x_r,
    hy_s,
    hy_r,
    mix_s,
    half_s,
    quarter_s,
    down_r,
    spread_s,
    spread_r,
):
    leaf = lax.axis_index("leaf")
    me = lax.axis_index("row")
    width = own.shape[0]
    owners = 2 * SEP // width
    near = leaf + 1 - 2 * lax.rem(leaf, 2)
    far = leaf + 2 - 4 * lax.rem(leaf // 2, 2)
    sibling = me + 1 - 2 * lax.rem(me, 2)
    tall = own.shape[1]
    short = tall - SEP

    barrier = pltpu.get_barrier_semaphore()
    for step in range(1, n_row):
        pl.semaphore_signal(
            barrier,
            inc=1,
            device_id={"leaf": leaf, "row": lax.rem(me + step, n_row)},
            device_id_type=MESH,
        )
    for other in (near, far):
        pl.semaphore_signal(
            barrier, inc=1, device_id={"leaf": other, "row": me}, device_id_type=MESH
        )
    pl.semaphore_wait(barrier, n_row + 1)

    def remote(src, dst, send, recv, to_leaf, to_row):
        return pltpu.make_async_remote_copy(
            src_ref=src,
            dst_ref=dst,
            send_sem=send,
            recv_sem=recv,
            device_id={"leaf": to_leaf, "row": to_row},
            device_id_type=MESH,
        )

    def rows_of(block):
        return short if block * width < SEP else tall

    def part_view(ref, block, part):
        return ref.at[pl.ds(part * (width // 2), width // 2), pl.ds(0, rows_of(block))]

    def raw(block, part, target):
        return remote(
            part_view(own, block, part),
            part_view(piv.at[block], block, part),
            raw_s.at[2 * target + part],
            raw_r.at[2 * block + part],
            leaf,
            target,
        )

    def pass_on(block, part, send, target):
        view = part_view(piv.at[block], block, part)
        return remote(view, view, send, raw_r.at[2 * block + part], leaf, target)

    def relay(block, part):
        return pass_on(block, part, relay_s.at[2 * block + part], sibling)

    def onward(block, part):
        return pass_on(block, part, onward_s.at[block], 6 + block % 2)

    square_plane = n_row == 8

    def raw_sends(block):
        chip, core = block // 2, block % 2
        sends = [(2 * chip + 1 - core, 0), (2 * chip + 1 - core, 1)]
        if square_plane:
            return sends + [(2 + core, 0), (4 + core, 1), (2 + core, 1), (4 + core, 0)]
        others = [2 * q + core for q in range(n_row // 2) if q != chip]
        return sends + [(target, part) for target in others for part in range(2)]

    def arrive(block, part):
        relay(block, part).wait_recv()

        @pl.when(lax.rem(me, 2) == block % 2)
        def _():
            relay(block, part).start()

        if square_plane:

            @pl.when(me == 2 + 2 * part + block % 2)
            def _():
                onward(block, part).start()

    def g_copy(i):
        return remote(gs.at[i], gr.at[i], g_s.at[i], g_r.at[i], near, me)

    mid = owners // 2

    for block in range(owners):

        @pl.when(me == block)
        def _():
            for target, part in raw_sends(block):
                raw(block, part, target).start()
            piv[block] = own[...]
            if block == 0 and mid == 1:
                gs[0] = dot(own[:, :short], own[:, :short], 1, 1)
                g_copy(0).start()

    for block in range(owners):

        @pl.when(me != block)
        def _():
            if square_plane:
                late = me == 4 + block % 2

                @pl.when(late)
                def _():
                    arrive(block, 1)
                    arrive(block, 0)

                @pl.when(jnp.logical_not(late))
                def _():
                    arrive(block, 0)
                    arrive(block, 1)

            else:
                arrive(block, 0)
                arrive(block, 1)

    def pivots(first, last, count):
        blocks = [piv[b, :, :count] for b in range(first, last)]
        return blocks[0] if len(blocks) == 1 else jnp.concatenate(blocks, axis=0)

    def x_copy(i):
        return remote(xs.at[i], xr.at[i], x_s.at[i], x_r.at[i], near, me)

    h_copy = remote(hs, hr, hy_s.at[0], hy_r.at[0], far, me)
    y_copy = remote(ys, yr, hy_s.at[1], hy_r.at[1], far, me)
    which_half = lax.rem(leaf, 2)
    which_quarter = lax.rem(leaf, 4)

    def mix_copy(target):
        return remote(mix, mix, mix_s.at[target], down_r.at[0], leaf, target)

    def half_copy(target):
        return remote(
            halves.at[which_half], half, half_s.at[target], down_r.at[1], leaf, target
        )

    def mix_relay():
        return remote(mix, mix, mix_s.at[0], down_r.at[0], leaf, sibling)

    def half_relay():
        return remote(half, half, half_s.at[0], down_r.at[1], leaf, sibling)

    relaying = jnp.logical_and(me != 0, lax.rem(me, 2) == 0)
    first_targets = [1] + list(range(2, n_row, 2))

    def quarter_copy(target):
        return remote(
            quarters.at[which_quarter], quarter, quarter_s.at[target], down_r.at[2], leaf, target
        )

    @pl.when(me == 0)
    def _():
        first = pivots(0, mid, short)
        if mid > 1:
            gs[0] = dot(first, first, 1, 1)
            g_copy(0).start()
        second = pivots(mid, owners, tall)
        gs[1] = dot(first, second[:, :short], 1, 1)
        g_copy(1).start()
        gs[2] = dot(second, second, 1, 1)
        g_copy(2).start()

    xs[0] = dot(own[:, :short], pivots(0, mid, short), 1, 1)
    x_copy(0).start()

    @pl.when(me >= mid)
    def _():
        xs[1] = dot(own[...], pivots(mid, owners, tall), 1, 1)
        x_copy(1).start()

    @pl.when(me == 0)
    def _():
        g_copy(0).wait_recv()
        inverse = factor_inverse(aug, gs[0] + gr[0])
        g_copy(1).wait_recv()
        pivot_rows = dot(inverse, gs[1] + gr[1], 1, 0)
        g_copy(2).wait_recv()
        hs[...] = gs[2] + gr[2] - dot(pivot_rows, pivot_rows, 0, 0)
        h_copy.start()
        mix[...] = dot(inverse, pivot_rows, 0, 0)
        for target in first_targets:
            mix_copy(target).start()
        halves[0] = inverse[: SEP // 2]
        halves[1] = inverse[SEP // 2 :]

    @pl.when(me != 0)
    def _():
        mix_copy(0).wait_recv()

    @pl.when(relaying)
    def _():
        mix_relay().start()

    x_copy(0).wait_recv()

    @pl.when(me >= mid)
    def _():
        correction = dot(xs[0] + xr[0], mix[...], 1, 0)
        x_copy(1).wait_recv()
        ys[...] = xs[1] + xr[1] - correction
        y_copy.start()

    @pl.when(me == 0)
    def _():
        h_copy.wait_recv()
        for target in first_targets:
            half_copy(target).start()
        inverse = factor_inverse(aug, hs[...] + hr[...])
        for i in range(4):
            quarters[i] = inverse[i * PANEL : (i + 1) * PANEL]
        for target in range(1, n_row):
            quarter_copy(target).start()
        half[...] = halves[which_half]
        quarter[...] = quarters[which_quarter]

    @pl.when(me != 0)
    def _():
        half_copy(0).wait_recv()

    @pl.when(relaying)
    def _():
        half_relay().start()

    four[...] = dot(xs[0] + xr[0], half[...], 1, 1)

    @pl.when(me != 0)
    def _():
        quarter_copy(0).wait_recv()

    share = PANEL // n_row

    @pl.when(me >= mid)
    def _():
        y_copy.wait_recv()
        spread = dot(quarter[...], ys[...] + yr[...], 1, 1)
        for target in range(n_row):
            ts[target] = spread[target * share : (target + 1) * share]

    def spread_copy(source, target):
        return remote(
            ts.at[target], tr.at[source], spread_s.at[target], spread_r.at[source], leaf, target
        )

    for target in range(n_row):

        @pl.when(jnp.logical_and(me >= mid, me != target))
        def _():
            spread_copy(me, target).start()

    for source in range(mid, n_row):

        @pl.when(me == source)
        def _():
            tr[source] = ts[source]

        @pl.when(me != source)
        def _():
            spread_copy(source, source).wait_recv()

    three[...] = jnp.concatenate([tr[source] for source in range(mid, n_row)], axis=1)

    for target in range(n_row):

        @pl.when(jnp.logical_and(me >= mid, me != target))
        def _():
            spread_copy(me, target).wait_send()

    for block in range(owners):

        @pl.when(me == block)
        def _():
            for target, part in raw_sends(block):
                raw(block, part, target).wait_send()

        @pl.when(jnp.logical_and(me != block, lax.rem(me, 2) == block % 2))
        def _():
            for part in range(2):
                relay(block, part).wait_send()

        if square_plane:
            for part in range(2):

                @pl.when(me == 2 + 2 * part + block % 2)
                def _():
                    onward(block, part).wait_send()

    x_copy(0).wait_send()

    @pl.when(me >= mid)
    def _():
        x_copy(1).wait_send()
        y_copy.wait_send()

    @pl.when(me == 0)
    def _():
        for i in range(3):
            g_copy(i).wait_send()
        h_copy.wait_send()
        for target in first_targets:
            mix_copy(target).wait_send()
            half_copy(target).wait_send()
        for target in range(1, n_row):
            quarter_copy(target).wait_send()

    @pl.when(relaying)
    def _():
        mix_relay().wait_send()
        half_relay().wait_send()


def fronts(own, n_row):
    width, tall = own.shape
    owners = 2 * SEP // width
    f32 = jnp.float32
    square = pltpu.VMEM((SEP, SEP), f32)
    dma = pltpu.SemaphoreType.DMA
    vmem = pl.BlockSpec(memory_space=pltpu.VMEM)
    return pl.pallas_call(
        functools.partial(kernel, n_row),
        out_shape=(
            jax.ShapeDtypeStruct((width, SEP // 2), f32),
            jax.ShapeDtypeStruct((SEP // 4 // n_row, width * n_row - SEP), f32),
        ),
        in_specs=[vmem],
        out_specs=(vmem, vmem),
        scratch_shapes=[
            pltpu.VMEM((owners, width, tall), f32),
            pltpu.VMEM((3, SEP, SEP), f32),
            pltpu.VMEM((3, SEP, SEP), f32),
            pltpu.VMEM((2, width, SEP), f32),
            pltpu.VMEM((2, width, SEP), f32),
            square,
            square,
            pltpu.VMEM((width, SEP), f32),
            pltpu.VMEM((width, SEP), f32),
            square,
            pltpu.VMEM((SEP // 2, SEP), f32),
            pltpu.VMEM((SEP // 4, SEP), f32),
            pltpu.VMEM((2, SEP // 2, SEP), f32),
            pltpu.VMEM((4, SEP // 4, SEP), f32),
            pltpu.VMEM((SEP, 2 * SEP), f32),
            pltpu.VMEM((n_row, SEP // 4 // n_row, width), f32),
            pltpu.VMEM((n_row, SEP // 4 // n_row, width), f32),
            dma((2 * n_row,)),
            dma((2 * owners,)),
            dma((2 * owners,)),
            dma((owners,)),
            dma((3,)),
            dma((3,)),
            dma((2,)),
            dma((2,)),
            dma((2,)),
            dma((2,)),
            dma((n_row,)),
            dma((n_row,)),
            dma((n_row,)),
            dma((3,)),
            dma((n_row,)),
            dma((n_row,)),
        ],
        compiler_params=pltpu.CompilerParams(
            collective_id=0, has_side_effects=True, vmem_limit_bytes=40 * 1024 * 1024
        ),
        name="fronts",
    )(own)


def masked_columns(values, pattern):
    col_blocks = pattern.shape[0]
    row_blocks = pattern.shape[1]
    blocks = values.reshape(col_blocks, PANEL, row_blocks, PANEL)
    flags = pattern[:, None, :, None].astype(jnp.float32)
    return (blocks * flags).reshape(values.shape)


def on_device(n_row, sub_factors, row_values, row_pattern):
    factors = sub_factors[0]
    assembled = masked_columns(row_values[0], row_pattern[0])
    own = jnp.concatenate([factors[:, :SEP], assembled, factors[:, SEP:]], axis=1)
    return fronts(own, n_row)


def solution(mesh):
    placed = (P("leaf", "row", None), P("leaf", "row", None), P("leaf", "row", None))
    return jax.shard_map(
        functools.partial(on_device, mesh.shape["row"]),
        mesh=mesh,
        in_specs=placed,
        out_specs=(P("row", "leaf"), P(("leaf", "row"), None)),
        check_vma=False,
    )
```
